32 devices in a mesh: ctx: 8 (over z, x), head: 4 (over y, core).
Axes of the slice: x: 2, y: 2, z: 4, core: 2. Of those that a mesh axis runs over, the one named last changes fastest.
Arguments:
- tokens: bfloat16 [2, 4096, 2048], P(None, 'ctx', 'head'), may hold values from -6 to 6
- region_lengths: int32 [2, 64], replicated, may hold values from 1 to 256, 4096 in all within a row
- header_lengths: int32 [2, 64], replicated, may hold values from 1 to 32
- w_query: bfloat16 [2048, 2048], P(None, 'head'), may hold values from -0.125 to 0.125
- w_key: bfloat16 [2048, 2048], P(None, 'head'), may hold values from -0.125 to 0.125
- w_value: bfloat16 [2048, 4096], P(None, 'head'), may hold values from -0.125 to 0.125
- w_gate: bfloat16 [2048, 4096], P(None, 'head'), may hold values from -0.125 to 0.125
- w_decay: bfloat16 [2048, 32], P(None, 'head'), may hold values from -0.125 to 0.125
- w_beta: bfloat16 [2048, 32], P(None, 'head'), may hold values from -0.125 to 0.125
- conv_query: float32 [4, 2048], P(None, 'head'), may hold values from -3 to 3
- conv_key: float32 [4, 2048], P(None, 'head'), may hold values from -3 to 3
- conv_value: float32 [4, 4096], P(None, 'head'), may hold values from -3 to 3
- decay_rate: float32 [32], P('head'), may hold values from 6.1035156e-05 to 0.1
- decay_bias: float32 [32], P('head'), may hold values from -2 to 1
- beta_bias: float32 [32], P('head'), may hold values from -6.5 to 1
- norm_gain: float32 [128], replicated, may hold values from 0.1 to 1.9
- w_out: bfloat16 [4096, 2048], P('head'), may hold values from -0.09375 to 0.09375
Outputs:
- mixed: bfloat16 [2, 4096, 2048], P(None, ('ctx', 'head'))
The draws below stay inside these ranges and needn't reach their ends.
Inputs may be any that keep to these rules, and one draw needn't show every extreme that they name: `region_lengths`: each row sums to 4096; the longest region has exactly 256 positions.
All inputs are finite; a program needn't handle non-finite values.
Results may differ from the reference program's by a relative error of at most 0.013.
Values may be sent and summed in bfloat16 or wider, within the bound.
A program may use at most 192 MiB of HBM per device.

```python
import math
import jax
import jax.numpy as jnp
import numpy as np
from jax import lax

D = 2048
QKH = 16
VH = 32
HD = 128
CONV = 4
GROUP = 64
SEQS = 2
REGIONS = 64
HDR = 32
LEN = 4096
RMOST = 256


def slow_heads(key, count):
    order = jax.random.permutation(key, VH)
    return order < count


def draw_decay_rate(key, part):
    count = VH // 4
    slow = slow_heads(key, count)
    key = jax.random.fold_in(key, 11)
    first_key, second_key = jax.random.split(key)
    quick = jnp.exp(jax.random.uniform(first_key, (VH,), jnp.float32, math.log(2.0 / LEN), math.log(0.1)))
    patient = jnp.exp(jax.random.uniform(second_key, (VH,), jnp.float32, math.log(0.25 / LEN), math.log(1.0 / LEN)))
    return jnp.where(slow, patient, quick).astype(jnp.float32)


def draw_beta_bias(key, part):
    count = VH // 4
    slow = slow_heads(key, count)
    key = jax.random.fold_in(key, 23)
    first_key, second_key = jax.random.split(key)
    drawn = jax.random.uniform(first_key, (VH,), jnp.float32, -1.0, 1.0)
    faint = jax.random.uniform(second_key, (VH,), jnp.float32, -6.5, -5.5)
    return jnp.where(slow, faint, drawn).astype(jnp.float32)


def place_ends(drawn, own_key, least, high):
    longest = drawn.shape.index(max(drawn.shape))
    spots = []
    for shift in (0, 1):
        where = [jax.random.randint(jax.random.fold_in(own_key, axis), (), 0, length) for axis, length in enumerate(drawn.shape)]
        where[longest] = (where[longest] + shift) % drawn.shape[longest]
        spots.append(tuple(where))
    return drawn.at[spots[0]].set(least).at[spots[1]].set(high)


def levels(rng, extent, cuts, smallest, largest):
    loudness, own = 1.0, jax.random.fold_in(rng, 6)
    for dim, parts in cuts:
        draws = jnp.exp(jax.random.uniform(jax.random.fold_in(own, dim), (parts,), jnp.float32, smallest / len(cuts), largest / len(cuts)))
        loudness = loudness * jnp.repeat(draws, extent[dim] // parts).reshape([-1 if axis == dim else 1 for axis in range(len(extent))])
    return loudness


def length_profile(amount, total, reach, skew):
    portions = [(1 << 20) // math.isqrt(grade ** skew) + 1 for grade in range(2, amount + 1)]
    rest, holding = total - reach - (amount - 1), [1] * (amount - 1)
    while rest > 0:
        candidates = [i for i in range(amount - 1) if holding[i] < reach]
        pool, budget = sum([portions[i] for i in candidates]), rest
        for i in candidates:
            more = min(reach - holding[i], max(1, budget * portions[i] // pool), rest)
            holding[i] = holding[i] + more
            rest = rest - more
    return np.array([reach] + holding)


def ragged_sizes(key, count, total, most, skew):
    if count == 2:
        one = jax.random.randint(key, (), max(1, total - most), min(most, total - 1) + 1)
        return jnp.stack([one, total - one])
    sizes = jnp.asarray(length_profile(count, total, most, skew), jnp.int32)
    pairs = (count - 1) // 2
    giver, taker = sizes[1:1 + 2 * pairs:2], sizes[2:2 + 2 * pairs:2]
    room = jnp.minimum(giver - 1, most - taker)
    passed = jax.random.randint(jax.random.fold_in(key, 1), (pairs,), 0, 1 << 20) % (room + 1)
    sizes = sizes.at[1:1 + 2 * pairs:2].set(giver - passed).at[2:2 + 2 * pairs:2].set(taker + passed)
    return sizes[jax.random.permutation(jax.random.fold_in(key, 2), count)]


def normal_values(own_key, shape, scale, reach, cuts=(), held_as=jnp.bfloat16):
    level = levels(own_key, shape, cuts, -0.22, 0.18) if cuts else 1.0
    values = jax.random.normal(own_key, shape, jnp.float32) * scale * level
    return jnp.minimum(jnp.maximum(values, -reach), reach).astype(held_as)


def setup_inputs(seed: int = 0) -> dict:
    key_of = jax.random.split(jax.random.key(seed), 18)
    tokens = normal_values(key_of[0], (SEQS, LEN, D), 1.0, 6.0, ((1, 8), (2, 4)))
    region_lengths = jax.vmap(lambda own: ragged_sizes(own, REGIONS, LEN, RMOST, 2))(jax.random.split(key_of[1], SEQS)).reshape((SEQS, REGIONS)).astype(jnp.int32)
    header_lengths = place_ends(jax.random.randint(key_of[2], (SEQS, REGIONS), 1, HDR + 1), jax.random.fold_in(key_of[2], 1), 1, HDR).astype(jnp.int32)
    w_query = normal_values(key_of[3], (D, QKH * HD), D ** -0.5, 0.125, ((1, 4),))
    w_key = normal_values(key_of[4], (D, QKH * HD), D ** -0.5, 0.125, ((1, 4),))
    w_value = normal_values(key_of[5], (D, VH * HD), D ** -0.5, 0.125, ((1, 4),))
    w_gate = normal_values(key_of[6], (D, VH * HD), D ** -0.5, 0.125, ((1, 4),))
    w_decay = normal_values(key_of[7], (D, VH), D ** -0.5, 0.125, ((1, 4),))
    w_beta = normal_values(key_of[8], (D, VH), D ** -0.5, 0.125, ((1, 4),))
    conv_query = normal_values(key_of[9], (CONV, QKH * HD), CONV ** -0.5, 3.0, ((1, 4),), jnp.float32)
    conv_key = normal_values(key_of[10], (CONV, QKH * HD), CONV ** -0.5, 3.0, ((1, 4),), jnp.float32)
    conv_value = normal_values(key_of[11], (CONV, VH * HD), CONV ** -0.5, 3.0, ((1, 4),), jnp.float32)
    decay_rate = draw_decay_rate(jax.random.fold_in(key_of[17], 71), 0)
    decay_bias = jnp.clip(-2.0 + 3.0 * jax.random.uniform(key_of[13], (VH,), jnp.float32) ** levels(key_of[13], (VH,), ((0, 4),), -0.2, 0.2), -2.0, 1.0)
    beta_bias = draw_beta_bias(jax.random.fold_in(key_of[17], 71), 0)
    norm_gain = jnp.clip(1.0 + 0.18 * jax.random.normal(key_of[15], (HD,), jnp.float32), 0.1, 1.9)
    w_out = normal_values(key_of[16], (VH * HD, D), (VH * HD) ** -0.5, 0.09375, ((0, 4),))
    return {"tokens": tokens, "region_lengths": region_lengths, "header_lengths": header_lengths, "w_query": w_query, "w_key": w_key, "w_value": w_value, "w_gate": w_gate, "w_decay": w_decay, "w_beta": w_beta, "conv_query": conv_query, "conv_key": conv_key, "conv_value": conv_value, "decay_rate": decay_rate, "decay_bias": decay_bias, "beta_bias": beta_bias, "norm_gain": norm_gain, "w_out": w_out}


HIGH = lax.Precision.HIGHEST

def product(form, left, right):
    return jnp.einsum(form, left, right, precision=HIGH)

def region_masks(position, region_lengths, header_lengths):
    ends = jnp.cumsum(region_lengths, axis=1)
    starts = ends - region_lengths
    span = jnp.minimum(header_lengths, region_lengths)
    inside = (position[None, None, :] >= starts[:, :, None]) & (position[None, None, :] < ends[:, :, None])
    header = inside & (position[None, None, :] < (starts + span)[:, :, None])
    return (inside, header, span)

def causal_conv(sequence, kernel, rim):
    extended = jnp.concatenate([rim, sequence], axis=1).astype(jnp.float32)
    width = kernel.shape[0]
    length = sequence.shape[1]
    total = kernel[0] * extended[:, 0:length]
    for offset in range(1, width):
        total = total + kernel[offset] * extended[:, offset:offset + length]
    return jax.nn.silu(total)

def unit_rows(rows, factor):
    return rows * lax.rsqrt(lax.optimization_barrier(jnp.sum(rows * rows, axis=-1, keepdims=True)) + 1e-06) * factor

def group_terms(queries, key_rows, value_rows, log_decay, strength):
    size = queries.shape[-2]
    dim_value = value_rows.shape[-1]
    dim_key = key_rows.shape[-1]
    cumul = jnp.cumsum(log_decay, axis=-1)
    places = jnp.arange(size)
    incl = places[:, None] >= places[None, :]
    strict = places[:, None] > places[None, :]
    spread = cumul[..., :, None] - cumul[..., None, :]
    ratio = jnp.where(incl, jnp.exp(jnp.where(incl, spread, 0.0)), 0.0)
    key_key = product('...td,...jd->...tj', key_rows, key_rows)
    lower = jnp.where(strict, ratio * key_key * strength[..., :, None], 0.0)
    system = lower + jnp.eye(size, dtype=jnp.float32)
    scaled = jnp.exp(cumul)[..., None]
    right_side = strength[..., None] * jnp.concatenate([value_rows, scaled * key_rows], axis=-1)
    solved = jax.scipy.linalg.solve_triangular(system, right_side, lower=True, unit_diagonal=True)
    local_u = solved[..., :dim_value]
    weights_w = solved[..., dim_value:]
    tail_keys = jnp.exp(cumul[..., -1:] - cumul)[..., None] * key_rows
    last_decay = jnp.exp(cumul[..., -1])
    transition = last_decay[..., None, None] * jnp.eye(dim_key, dtype=jnp.float32) - product('...td,...te->...de', tail_keys, weights_w)
    offset_map = product('...td,...te->...de', tail_keys, local_u)
    attend = ratio * product('...td,...jd->...tj', queries, key_rows)
    query_eff = scaled * queries - product('...tj,...jd->...td', attend, weights_w)
    base_out = product('...tj,...jd->...td', attend, local_u)
    return (transition, offset_map, query_eff, base_out)

def gated_norm(outputs, gate_raw, norm_gain):
    mean_sq = lax.optimization_barrier(jnp.mean(outputs * outputs, axis=-1, keepdims=True))
    gate_val = jax.nn.silu(gate_raw.astype(jnp.float32))
    return outputs * lax.rsqrt(mean_sq + 1e-06) * norm_gain * gate_val

def head_path(inputs):
    queries, key_rows, value_rows, log_decay, strength = inputs
    seq_count, length, head_dim = queries.shape
    blocks = length // GROUP

    def cut(array):
        return array.reshape((seq_count, blocks, GROUP) + array.shape[2:])
    transition, offset_map, query_eff, base_out = group_terms(cut(queries), cut(key_rows), cut(value_rows), cut(log_decay), cut(strength))

    def advance(state, items):
        trans_now, offset_now, query_now, base_now = items
        result = product('std,sde->ste', query_now, state) + base_now
        return (product('sde,sef->sdf', trans_now, state) + offset_now, result)
    start_state = jnp.zeros((seq_count, head_dim, head_dim), jnp.float32)
    moved = tuple((jnp.moveaxis(item, 1, 0) for item in (transition, offset_map, query_eff, base_out)))
    _, results = lax.scan(advance, start_state, moved)
    return jnp.moveaxis(results, 0, 1).reshape(seq_count, length, head_dim)

def reference(tokens, region_lengths, header_lengths, w_query, w_key, w_value, w_gate, w_decay, w_beta, conv_query, conv_key, conv_value, decay_rate, decay_bias, beta_bias, norm_gain, w_out):
    seq_count, length, width = tokens.shape
    position = jnp.arange(length, dtype=jnp.int32)
    inside, header, span = region_masks(position, region_lengths, header_lengths)
    tokens_wide = tokens.astype(jnp.float32)
    sums = product('srt,std->srd', header.astype(jnp.float32), tokens_wide)
    means = sums / span[..., None].astype(jnp.float32)
    augmented = (tokens_wide + product('srt,srd->std', inside.astype(jnp.float32), means)).astype(jnp.bfloat16)
    flat = augmented.reshape(seq_count * length, width)

    def project(weight):
        return jnp.dot(flat.astype(jnp.float32), weight.astype(jnp.float32), preferred_element_type=jnp.float32).reshape(seq_count, length, weight.shape[1])
    query_raw = project(w_query).astype(jnp.bfloat16)
    key_raw = project(w_key).astype(jnp.bfloat16)
    value_raw = project(w_value).astype(jnp.bfloat16)
    gate_raw = project(w_gate).astype(jnp.bfloat16)
    decay_logit = project(w_decay)
    beta_logit = project(w_beta)

    def convolve(raw, kernel):
        rim = jnp.zeros((seq_count, CONV - 1, raw.shape[2]), jnp.bfloat16)
        return causal_conv(raw, kernel, rim)
    queries = unit_rows(convolve(query_raw, conv_query).reshape(seq_count, length, QKH, HD), HD ** (-0.5))
    key_rows = unit_rows(convolve(key_raw, conv_key).reshape(seq_count, length, QKH, HD), 1.0)
    value_rows = convolve(value_raw, conv_value).reshape(seq_count, length, VH, HD)
    queries = jnp.repeat(queries, 2, axis=2)
    key_rows = jnp.repeat(key_rows, 2, axis=2)
    log_decay = -decay_rate * jax.nn.softplus(decay_logit + decay_bias)
    strength = jax.nn.sigmoid(beta_logit + beta_bias)
    stacked = (jnp.moveaxis(queries, 2, 0), jnp.moveaxis(key_rows, 2, 0), jnp.moveaxis(value_rows, 2, 0), jnp.moveaxis(log_decay, 2, 0), jnp.moveaxis(strength, 2, 0))
    outputs = jnp.moveaxis(lax.map(head_path, stacked), 0, 2)
    normed = gated_norm(outputs, gate_raw.reshape(seq_count, length, VH, HD), norm_gain)
    hidden = normed.astype(jnp.bfloat16).reshape(seq_count * length, VH * HD)
    mixed = jnp.dot(hidden.astype(jnp.float32), w_out.astype(jnp.float32), preferred_element_type=jnp.float32)
    return mixed.reshape(seq_count, length, width).astype(jnp.bfloat16)
```

```python
import jax
import jax.numpy as jnp
from jax import lax
from jax.experimental import pallas as pl
from jax.experimental.pallas import tpu as pltpu
from jax.sharding import PartitionSpec as P

CHUNK = 128
HIGH = lax.Precision.HIGHEST
BF16 = jnp.bfloat16
F32 = jnp.float32


def shifted(shard, axis, by):
    length = lax.axis_size(axis)
    pairs = [(i, i + by) for i in range(length) if 0 <= i + by < length]
    return lax.ppermute(shard, axis, pairs)


def dot(left, right):
    return jnp.dot(left.astype(BF16), right.astype(BF16), preferred_element_type=F32)


def silu(x):
    return x * (0.5 + 0.5 * jnp.tanh(0.5 * x))


def unit_inverses(lowers):
    size = lowers[0].shape[0]
    row = lax.broadcasted_iota(jnp.int32, (size, size), 0)
    col = lax.broadcasted_iota(jnp.int32, (size, size), 1)
    eye = (row == col).astype(F32)
    pair = (row // 2 == col // 2).astype(F32)
    inverses = [eye - pair * lower for lower in lowers]
    half = 2
    while half < size:
        below = ((row // (2 * half) == col // (2 * half)) & (row // half != col // half)).astype(F32)
        halves = [inverse.astype(BF16) for inverse in inverses]
        inner = [dot(lower * below, inverse) for lower, inverse in zip(lowers, halves)]
        outer = [dot(inverse, term) for inverse, term in zip(halves, inner)]
        inverses = [inverse - term for inverse, term in zip(inverses, outer)]
        half *= 2
    return inverses


def delta_kernel(
    q_ref, k_ref, v_ref, rq_ref, rk_ref, rv_ref, tq_ref, tk_ref, tv_ref, col_ref, row_ref,
    state_ref, query_ref, base_ref, scr,
):
    tok = q_ref.shape[1]
    dim = q_ref.shape[2]
    share = v_ref.shape[2] // dim
    chunks = tok // CHUNK

    def conv(raw_ref, rim_ref, taps_ref, which):
        lanes = slice(which * dim, (which + 1) * dim)
        scr[0:8, :] = rim_ref[0, :, lanes]
        scr[8 : 8 + tok, :] = raw_ref[0, :, lanes].astype(F32)
        total = taps_ref[0:1, lanes] * scr[5 : 5 + tok, :]
        for i in range(1, 4):
            total = total + taps_ref[i : i + 1, lanes] * scr[5 + i : 5 + i + tok, :]
        return silu(total)

    queries = conv(q_ref, rq_ref, tq_ref, 0)
    queries = queries * (
        lax.rsqrt(jnp.sum(queries * queries, axis=-1, keepdims=True) + 1e-06) * dim ** (-0.5)
    )
    keys = conv(k_ref, rk_ref, tk_ref, 0)
    keys = keys * lax.rsqrt(jnp.sum(keys * keys, axis=-1, keepdims=True) + 1e-06)
    values = [conv(v_ref, rv_ref, tv_ref, j) for j in range(share)]

    row = lax.broadcasted_iota(jnp.int32, (CHUNK, CHUNK), 0)
    col = lax.broadcasted_iota(jnp.int32, (CHUNK, CHUNK), 1)
    incl = row >= col
    strict = row > col
    units = [(c, j) for c in range(chunks) for j in range(share)]
    lowers, attends, rights, sides, tails, decays = [], [], [], [], [], []
    for c in range(chunks):
        span = slice(c * CHUNK, (c + 1) * CHUNK)
        qc = queries[span]
        kc = keys[span]
        both = jnp.concatenate([qc, kc], axis=0).astype(BF16)
        kt = kc.T
        gram = dot(both, kt)
        for j in range(share):
            cc = col_ref[0, 0, span, j : j + 1]
            bc = col_ref[0, 0, span, share + j : share + j + 1]
            cr = row_ref[0, 0, j : j + 1, span]
            last = row_ref[0, 0, j : j + 1, (c + 1) * CHUNK - 1 : (c + 1) * CHUNK]
            ratio = jnp.where(incl, jnp.exp(jnp.minimum(cc - cr, 0.0)), 0.0)
            lowers.append(jnp.where(strict, ratio * gram[CHUNK:] * bc, 0.0))
            scaled = jnp.exp(cc)
            rights.append(
                jnp.concatenate([bc * values[j][span], (bc * scaled) * kc], axis=1).astype(BF16)
            )
            attends.append(
                jnp.concatenate([ratio * gram[:CHUNK], jnp.exp(last - cr) * kt], axis=0).astype(BF16)
            )
            sides.append((scaled * qc).astype(BF16))
            decays.append(jnp.exp(last))
    inverses = unit_inverses(lowers)
    solved = [dot(inverse, right) for inverse, right in zip(inverses, rights)]

    eye = (row == col).astype(F32)
    zero = jnp.zeros((CHUNK, dim), F32)
    states = [jnp.concatenate([eye, zero], axis=1) for _ in range(share)]
    for c in range(chunks):
        span = slice(c * CHUNK, (c + 1) * CHUNK)
        for j in range(share):
            u = c * share + j
            local = solved[u][:, :dim]
            left = jnp.concatenate([solved[u][:, dim:].astype(BF16), sides[u]], axis=0)
            seen = dot(left, states[j])
            delta = jnp.concatenate([zero, local], axis=1) - seen[:CHUNK]
            moved = dot(attends[u], delta)
            out = seen[CHUNK:] + moved[:CHUNK]
            states[j] = decays[u] * states[j] + moved[CHUNK:]
            lanes = slice(j * dim, (j + 1) * dim)
            query_ref[0, span, lanes] = out[:, :dim].astype(BF16)
            base_ref[0, span, lanes] = out[:, dim:]
    for j in range(share):
        state_ref[0, j] = states[j].astype(BF16)


def delta_local(q, k, v, rims, taps, cols, rows, dim):
    seqs, tok, qk_width = q.shape
    groups = qk_width // dim
    share = v.shape[2] // qk_width
    wide = share * dim
    narrow = pl.BlockSpec((1, tok, dim), lambda s, g: (s, 0, g))
    broad = pl.BlockSpec((1, tok, wide), lambda s, g: (s, 0, g))
    return pl.pallas_call(
        delta_kernel,
        grid=(seqs, groups),
        in_specs=[
            narrow,
            narrow,
            broad,
            pl.BlockSpec((1, 8, dim), lambda s, g: (s, 0, g)),
            pl.BlockSpec((1, 8, dim), lambda s, g: (s, 0, g)),
            pl.BlockSpec((1, 8, wide), lambda s, g: (s, 0, g)),
            pl.BlockSpec((4, dim), lambda s, g: (0, g)),
            pl.BlockSpec((4, dim), lambda s, g: (0, g)),
            pl.BlockSpec((4, wide), lambda s, g: (0, g)),
            pl.BlockSpec((1, 1, tok, 2 * share), lambda s, g: (g, s, 0, 0)),
            pl.BlockSpec((1, 1, share, tok), lambda s, g: (g, s, 0, 0)),
        ],
        out_specs=[
            pl.BlockSpec((1, share, dim, 2 * dim), lambda s, g: (s, g, 0, 0)),
            broad,
            broad,
        ],
        out_shape=[
            jax.ShapeDtypeStruct((seqs, groups * share, dim, 2 * dim), BF16),
            jax.ShapeDtypeStruct(v.shape, BF16),
            jax.ShapeDtypeStruct(v.shape, F32),
        ],
        scratch_shapes=[pltpu.VMEM((tok + 8, dim), F32)],
        compiler_params=pltpu.CompilerParams(vmem_limit_bytes=40 << 20),
        cost_estimate=pl.CostEstimate(
            flops=40 * seqs * tok * v.shape[2] * dim, bytes_accessed=16 << 20, transcendentals=0
        ),
    )(q, k, v, *rims, *taps, cols, rows)


def prefix_kernel(maps_ref, out_ref):
    steps, chains, dim, _ = maps_ref.shape
    states = [jnp.zeros((dim, dim), F32) for _ in range(chains)]
    for step in range(steps):
        for c in range(chains):
            out_ref[step, c] = states[c].astype(BF16)
            if step < steps - 1:
                now = maps_ref[step, c, :, :dim]
                top = states[c].astype(BF16)
                rest = states[c] - top.astype(F32)
                states[c] = maps_ref[step, c, :, dim:].astype(F32) + dot(now, top) + dot(now, rest)


def prefix_states(maps):
    steps, chains, dim, _ = maps.shape
    return pl.pallas_call(
        prefix_kernel,
        out_shape=jax.ShapeDtypeStruct((steps, chains, dim, dim), BF16),
        compiler_params=pltpu.CompilerParams(vmem_limit_bytes=24 << 20),
    )(maps)


def finish_kernel(query_ref, base_ref, gate_ref, state_ref, gain_ref, out_ref):
    dim = gain_ref.shape[1]
    for j in range(out_ref.shape[1] // dim):
        lanes = slice(j * dim, (j + 1) * dim)
        out = dot(query_ref[0, :, lanes], state_ref[0, j]) + base_ref[0, :, lanes]
        mean_sq = jnp.mean(out * out, axis=-1, keepdims=True)
        gate = silu(gate_ref[0, :, lanes].astype(F32))
        out_ref[:, lanes] = (out * lax.rsqrt(mean_sq + 1e-06) * gain_ref[...] * gate).astype(BF16)


def finish(query, base, gate, states, gain, seq):
    tok, width = query.shape[1:]
    dim = gain.shape[0]
    share = 2
    wide = share * dim
    broad = pl.BlockSpec((1, tok, wide), lambda g: (seq, 0, g))
    return pl.pallas_call(
        finish_kernel,
        grid=(width // wide,),
        in_specs=[
            broad,
            broad,
            broad,
            pl.BlockSpec((1, share, dim, dim), lambda g: (seq, g, 0, 0)),
            pl.BlockSpec((1, dim), lambda g: (0, 0)),
        ],
        out_specs=pl.BlockSpec((tok, wide), lambda g: (0, g)),
        out_shape=jax.ShapeDtypeStruct((tok, width), BF16),
        compiler_params=pltpu.CompilerParams(vmem_limit_bytes=24 << 20),
    )(query, base, gate, states, gain.reshape(1, dim))


def augment(tokens, region_lengths, header_lengths):
    tok = tokens.shape[1]
    place = lax.axis_index("ctx")
    parts = lax.axis_size("ctx")
    longest = tok * parts // 16
    hops = -(-(longest - 1) // tok)
    position = place * tok + jnp.arange(tok, dtype=jnp.int32)
    ends = jnp.cumsum(region_lengths, axis=1)
    starts = ends - region_lengths
    span = jnp.minimum(header_lengths, region_lengths)
    inside = (position[None, None, :] >= starts[:, :, None]) & (
        position[None, None, :] < ends[:, :, None]
    )
    header = inside & (position[None, None, :] < (starts + span)[:, :, None])

    def holds(point):
        return ((starts <= point) & (point < ends))[:, :, None]

    sums = jnp.einsum("srt,std->srd", header.astype(BF16), tokens, preferred_element_type=F32)

    def part_at(point):
        return jnp.sum(jnp.where(holds(point), sums, 0.0), axis=1)

    before = shifted(part_at((place + 1) * tok), "ctx", 1)
    for hop in range(2, hops + 1):
        before = before + shifted(part_at((place + hop) * tok), "ctx", hop)
    after = shifted(part_at(place * tok), "ctx", -1)
    totals = (
        sums
        + jnp.where(holds(place * tok), before[:, None, :], 0.0)
        + jnp.where(holds((place + 1) * tok), after[:, None, :], 0.0)
    )
    means = totals / span[..., None].astype(F32)
    top = means.astype(BF16)
    rest = (means - top.astype(F32)).astype(BF16)
    spread = inside.astype(BF16)
    added = jnp.einsum(
        "srt,srd->std",
        jnp.concatenate([spread, spread], axis=1),
        jnp.concatenate([top, rest], axis=1),
        preferred_element_type=F32,
    )
    return (tokens.astype(F32) + added).astype(BF16)


def incoming_states(maps, dim):
    seqs, heads = maps.shape[:2]
    parts = lax.axis_size("ctx")
    chains = seqs * heads
    if chains % parts == 0:
        sent = maps.reshape(parts, chains // parts, dim, 2 * dim)
        held = lax.all_to_all(sent, "ctx", 0, 0, tiled=True)
        states = lax.all_to_all(prefix_states(held), "ctx", 0, 0, tiled=True)
        return states.reshape(seqs, heads, dim, dim)

    def relay(counter, state):
        moved = jnp.einsum(
            "shde,shef->shdf", maps[..., :dim], state, preferred_element_type=F32
        ) + maps[..., dim:].astype(F32)
        return shifted(moved.astype(BF16), "ctx", 1)

    return lax.fori_loop(0, parts - 1, relay, jnp.zeros((seqs, heads, dim, dim), BF16))


def per_device(
    tokens,
    region_lengths,
    header_lengths,
    w_query,
    w_key,
    w_value,
    w_gate,
    w_decay,
    w_beta,
    conv_query,
    conv_key,
    conv_value,
    decay_rate,
    decay_bias,
    beta_bias,
    norm_gain,
    w_out,
):
    seqs, tok, _ = tokens.shape
    dim = norm_gain.shape[0]
    heads = w_decay.shape[1]
    groups = w_query.shape[1] // dim
    share = heads // groups
    chunks = tok // CHUNK
    augmented = augment(tokens, region_lengths, header_lengths)
    whole = lax.all_gather(augmented, "head", axis=2, tiled=True)

    def project(weight):
        return jnp.einsum("std,de->ste", whole, weight, preferred_element_type=F32)

    raws = [project(weight).astype(BF16) for weight in (w_query, w_key, w_value)]
    rim = shifted(jnp.concatenate([raw[:, tok - 3 :, :] for raw in raws], axis=-1), "ctx", 1)
    gate_raw = project(w_gate).astype(BF16)
    small = project(jnp.concatenate([w_decay, w_beta], axis=1))
    log_decay = -decay_rate * jax.nn.softplus(small[..., :heads] + decay_bias)
    strength = jax.nn.sigmoid(small[..., heads:] + beta_bias)
    places = jnp.arange(CHUNK)
    below = (places[:, None] >= places[None, :]).astype(F32)
    cumul = jnp.einsum(
        "ij,scjh->scih", below, log_decay.reshape(seqs, chunks, CHUNK, heads), precision=HIGH
    ).reshape(seqs, tok, groups, share)
    strength = strength.reshape(seqs, tok, groups, share)
    cols = jnp.concatenate([cumul, strength], axis=-1).transpose(2, 0, 1, 3)
    rows = cumul.transpose(2, 0, 3, 1)
    rim = jnp.pad(rim.astype(F32), ((0, 0), (5, 0), (0, 0)))
    width = groups * dim
    rims = (rim[..., :width], rim[..., width : 2 * width], rim[..., 2 * width :])
    maps, query_total, base_total = delta_local(
        *raws, rims, (conv_query, conv_key, conv_value), cols, rows, dim
    )
    states = incoming_states(maps, dim)
    mixed = []
    for seq in range(seqs):
        hidden = finish(query_total, base_total, gate_raw, states, norm_gain, seq)
        partial = jnp.dot(hidden, w_out, preferred_element_type=F32).astype(BF16)
        mixed.append(lax.psum_scatter(partial, "head", scatter_dimension=0, tiled=True))
    return jnp.stack(mixed)


def solution(mesh):
    return jax.shard_map(
        per_device,
        mesh=mesh,
        in_specs=(
            P(None, "ctx", "head"),
            P(),
            P(),
            P(None, "head"),
            P(None, "head"),
            P(None, "head"),
            P(None, "head"),
            P(None, "head"),
            P(None, "head"),
            P(None, "head"),
            P(None, "head"),
            P(None, "head"),
            P("head"),
            P("head"),
            P("head"),
            P(),
            P("head", None),
        ),
        out_specs=P(None, ("ctx", "head"), None),
        check_vma=False,
    )
```

```python
import jax
import jax.numpy as jnp
from jax import lax
from jax.experimental import pallas as pl
from jax.experimental.pallas import tpu as pltpu
from jax.sharding import PartitionSpec as P

CHUNK = 128
HIGH = lax.Precision.HIGHEST
BF16 = jnp.bfloat16
F32 = jnp.float32


def shifted(shard, axis, by):
    length = lax.axis_size(axis)
    pairs = [(i, i + by) for i in range(length) if 0 <= i + by < length]
    return lax.ppermute(shard, axis, pairs)


def dot(left, right):
    return jnp.dot(left.astype(BF16), right.astype(BF16), preferred_element_type=F32)


def silu(x):
    return x * (0.5 + 0.5 * jnp.tanh(0.5 * x))


def unit_inverses(lowers):
    size = lowers[0].shape[0]
    row = lax.broadcasted_iota(jnp.int32, (size, size), 0)
    col = lax.broadcasted_iota(jnp.int32, (size, size), 1)
    eye = (row == col).astype(F32)
    pair = (row // 2 == col // 2).astype(F32)
    inverses = [eye - pair * lower for lower in lowers]
    half = 2
    while half < size:
        below = ((row // (2 * half) == col // (2 * half)) & (row // half != col // half)).astype(F32)
        halves = [inverse.astype(BF16) for inverse in inverses]
        inner = [dot(lower * below, inverse) for lower, inverse in zip(lowers, halves)]
        outer = [dot(inverse, term) for inverse, term in zip(halves, inner)]
        inverses = [inverse - term for inverse, term in zip(inverses, outer)]
        half *= 2
    return inverses


def delta_kernel(
    q_ref, k_ref, v_ref, rq_ref, rk_ref, rv_ref, tq_ref, tk_ref, tv_ref, col_ref, row_ref,
    state_ref, query_ref, base_ref, scr,
):
    tok, dim = q_ref.shape
    share = v_ref.shape[1] // dim
    chunks = tok // CHUNK

    def conv(raw_ref, rim_ref, taps_ref, which):
        lanes = slice(which * dim, (which + 1) * dim)
        scr[0:8, :] = rim_ref[:, lanes]
        scr[8 : 8 + tok, :] = raw_ref[:, lanes].astype(F32)
        total = taps_ref[0:1, lanes] * scr[5 : 5 + tok, :]
        for i in range(1, 4):
            total = total + taps_ref[i : i + 1, lanes] * scr[5 + i : 5 + i + tok, :]
        return silu(total)

    queries = conv(q_ref, rq_ref, tq_ref, 0)
    queries = queries * (
        lax.rsqrt(jnp.sum(queries * queries, axis=-1, keepdims=True) + 1e-06) * dim ** (-0.5)
    )
    keys = conv(k_ref, rk_ref, tk_ref, 0)
    keys = keys * lax.rsqrt(jnp.sum(keys * keys, axis=-1, keepdims=True) + 1e-06)
    values = [conv(v_ref, rv_ref, tv_ref, j) for j in range(share)]

    row = lax.broadcasted_iota(jnp.int32, (CHUNK, CHUNK), 0)
    col = lax.broadcasted_iota(jnp.int32, (CHUNK, CHUNK), 1)
    incl = row >= col
    strict = row > col
    units = [(c, j) for c in range(chunks) for j in range(share)]
    lowers, attends, rights, sides, tails, decays = [], [], [], [], [], []
    for c in range(chunks):
        span = slice(c * CHUNK, (c + 1) * CHUNK)
        qc = queries[span]
        kc = keys[span]
        both = jnp.concatenate([qc, kc], axis=0).astype(BF16)
        kt = kc.T
        gram = dot(both, kt)
        for j in range(share):
            cc = col_ref[0, span, j : j + 1]
            bc = col_ref[0, span, share + j : share + j + 1]
            cr = row_ref[0, j : j + 1, span]
            last = row_ref[0, j : j + 1, (c + 1) * CHUNK - 1 : (c + 1) * CHUNK]
            ratio = jnp.where(incl, jnp.exp(jnp.minimum(cc - cr, 0.0)), 0.0)
            lowers.append(jnp.where(strict, ratio * gram[CHUNK:] * bc, 0.0))
            scaled = jnp.exp(cc)
            rights.append(
                jnp.concatenate([bc * values[j][span], (bc * scaled) * kc], axis=1).astype(BF16)
            )
            attends.append(
                jnp.concatenate([ratio * gram[:CHUNK], jnp.exp(last - cr) * kt], axis=0).astype(BF16)
            )
            sides.append((scaled * qc).astype(BF16))
            decays.append(jnp.exp(last))
    inverses = unit_inverses(lowers)
    solved = [dot(inverse, right) for inverse, right in zip(inverses, rights)]

    eye = (row == col).astype(F32)
    zero = jnp.zeros((CHUNK, dim), F32)
    states = [jnp.concatenate([eye, zero], axis=1) for _ in range(share)]
    for c in range(chunks):
        span = slice(c * CHUNK, (c + 1) * CHUNK)
        for j in range(share):
            u = c * share + j
            local = solved[u][:, :dim]
            left = jnp.concatenate([solved[u][:, dim:].astype(BF16), sides[u]], axis=0)
            seen = dot(left, states[j])
            delta = jnp.concatenate([zero, local], axis=1) - seen[:CHUNK]
            moved = dot(attends[u], delta)
            out = seen[CHUNK:] + moved[:CHUNK]
            states[j] = decays[u] * states[j] + moved[CHUNK:]
            lanes = slice(j * dim, (j + 1) * dim)
            query_ref[span, lanes] = out[:, :dim].astype(BF16)
            base_ref[span, lanes] = out[:, dim:]
    for j in range(share):
        state_ref[j] = states[j].astype(BF16)


def delta_local(q, k, v, rims, taps, cols, rows, dim):
    tok, qk_width = q.shape
    groups = qk_width // dim
    share = v.shape[1] // qk_width
    wide = share * dim
    narrow = pl.BlockSpec((tok, dim), lambda g: (0, g))
    broad = pl.BlockSpec((tok, wide), lambda g: (0, g))
    return pl.pallas_call(
        delta_kernel,
        grid=(groups,),
        in_specs=[
            narrow,
            narrow,
            broad,
            pl.BlockSpec((8, dim), lambda g: (0, g)),
            pl.BlockSpec((8, dim), lambda g: (0, g)),
            pl.BlockSpec((8, wide), lambda g: (0, g)),
            pl.BlockSpec((4, dim), lambda g: (0, g)),
            pl.BlockSpec((4, dim), lambda g: (0, g)),
            pl.BlockSpec((4, wide), lambda g: (0, g)),
            pl.BlockSpec((1, tok, 2 * share), lambda g: (g, 0, 0)),
            pl.BlockSpec((1, share, tok), lambda g: (g, 0, 0)),
        ],
        out_specs=[
            pl.BlockSpec((share, dim, 2 * dim), lambda g: (g, 0, 0)),
            broad,
            broad,
        ],
        out_shape=[
            jax.ShapeDtypeStruct((groups * share, dim, 2 * dim), BF16),
            jax.ShapeDtypeStruct(v.shape, BF16),
            jax.ShapeDtypeStruct(v.shape, F32),
        ],
        scratch_shapes=[pltpu.VMEM((tok + 8, dim), F32)],
        compiler_params=pltpu.CompilerParams(vmem_limit_bytes=48 << 20),
        cost_estimate=pl.CostEstimate(
            flops=300 * tok * v.shape[1] * dim, bytes_accessed=8 << 20, transcendentals=0
        ),
    )(q, k, v, *rims, *taps, cols, rows)


def prefix_kernel(maps_ref, out_ref):
    steps, chains, dim, _ = maps_ref.shape
    states = [jnp.zeros((dim, dim), F32) for _ in range(chains)]
    for step in range(steps):
        for c in range(chains):
            out_ref[step, c] = states[c].astype(BF16)
            if step < steps - 1:
                now = maps_ref[step, c, :, :dim]
                top = states[c].astype(BF16)
                rest = states[c] - top.astype(F32)
                states[c] = maps_ref[step, c, :, dim:].astype(F32) + dot(now, top) + dot(now, rest)


def prefix_states(maps):
    steps, chains, dim, _ = maps.shape
    return pl.pallas_call(
        prefix_kernel,
        out_shape=jax.ShapeDtypeStruct((steps, chains, dim, dim), BF16),
        compiler_params=pltpu.CompilerParams(vmem_limit_bytes=24 << 20),
    )(maps)


def finish_kernel(query_ref, base_ref, gate_ref, state_ref, gain_ref, out_ref):
    dim = gain_ref.shape[1]
    for j in range(out_ref.shape[1] // dim):
        lanes = slice(j * dim, (j + 1) * dim)
        out = dot(query_ref[:, lanes], state_ref[j]) + base_ref[:, lanes]
        mean_sq = jnp.mean(out * out, axis=-1, keepdims=True)
        gate = silu(gate_ref[:, lanes].astype(F32))
        out_ref[:, lanes] = (out * lax.rsqrt(mean_sq + 1e-06) * gain_ref[...] * gate).astype(BF16)


def finish(query, base, gate, states, gain):
    tok, width = query.shape
    dim = gain.shape[0]
    share = 2
    wide = share * dim
    broad = pl.BlockSpec((tok, wide), lambda g: (0, g))
    return pl.pallas_call(
        finish_kernel,
        grid=(width // wide,),
        in_specs=[
            broad,
            broad,
            broad,
            pl.BlockSpec((share, dim, dim), lambda g: (g, 0, 0)),
            pl.BlockSpec((1, dim), lambda g: (0, 0)),
        ],
        out_specs=broad,
        out_shape=jax.ShapeDtypeStruct((tok, width), BF16),
        compiler_params=pltpu.CompilerParams(vmem_limit_bytes=48 << 20),
        cost_estimate=pl.CostEstimate(flops=1 << 31, bytes_accessed=8 << 20, transcendentals=0),
    )(query, base, gate, states, gain.reshape(1, dim))


def augment(tokens, lengths, headers):
    tok = tokens.shape[0]
    place = lax.axis_index("ctx")
    parts = lax.axis_size("ctx")
    longest = tok * parts // 16
    hops = -(-(longest - 1) // tok)
    position = place * tok + jnp.arange(tok, dtype=jnp.int32)
    ends = jnp.cumsum(lengths)
    starts = ends - lengths
    span = jnp.minimum(headers, lengths)
    inside = (position[None, :] >= starts[:, None]) & (position[None, :] < ends[:, None])
    header = inside & (position[None, :] < (starts + span)[:, None])

    def holds(point):
        return ((starts <= point) & (point < ends))[:, None]

    sums = jnp.einsum("rt,td->rd", header.astype(BF16), tokens, preferred_element_type=F32)

    def part_at(point):
        return jnp.sum(jnp.where(holds(point), sums, 0.0), axis=0, keepdims=True)

    before = shifted(part_at((place + 1) * tok), "ctx", 1)
    for hop in range(2, hops + 1):
        before = before + shifted(part_at((place + hop) * tok), "ctx", hop)
    after = shifted(part_at(place * tok), "ctx", -1)
    totals = (
        sums
        + jnp.where(holds(place * tok), before, 0.0)
        + jnp.where(holds((place + 1) * tok), after, 0.0)
    )
    means = totals / span[:, None].astype(F32)
    top = means.astype(BF16)
    rest = (means - top.astype(F32)).astype(BF16)
    spread = inside.astype(BF16)
    added = jnp.einsum(
        "rt,rd->td",
        jnp.concatenate([spread, spread], axis=0),
        jnp.concatenate([top, rest], axis=0),
        preferred_element_type=F32,
    )
    return (tokens.astype(F32) + added).astype(BF16)


def incoming_states(maps, dim):
    heads = maps.shape[0]
    parts = lax.axis_size("ctx")
    if heads % parts == 0:
        sent = maps.reshape(parts, heads // parts, dim, 2 * dim)
        held = lax.all_to_all(sent, "ctx", 0, 0, tiled=True)
        states = lax.all_to_all(prefix_states(held), "ctx", 0, 0, tiled=True)
        return states.reshape(heads, dim, dim)

    def relay(counter, state):
        moved = jnp.einsum(
            "hde,hef->hdf", maps[..., :dim], state, preferred_element_type=F32
        ) + maps[..., dim:].astype(F32)
        return shifted(moved.astype(BF16), "ctx", 1)

    return lax.fori_loop(0, parts - 1, relay, jnp.zeros((heads, dim, dim), BF16))


def head_sum(hidden, w_out):
    size = lax.axis_size("head")
    me = lax.axis_index("head")
    chips = size // 2
    core, chip = me % 2, me // 2
    rows = hidden.shape[0] // size
    cut = hidden.reshape(chips, 2, rows, hidden.shape[1])

    def half(which):
        picked = lax.dynamic_index_in_dim(cut, which, 1, keepdims=False)
        return jnp.dot(
            picked.reshape(chips * rows, hidden.shape[1]), w_out, preferred_element_type=F32
        ).astype(BF16)

    arrived = lax.ppermute(half(1 - core), "head", [(i, i ^ 1) for i in range(size)])
    both = half(core).astype(F32) + arrived.astype(F32)
    both = both.reshape(chips, rows, w_out.shape[1])
    total = lax.dynamic_index_in_dim(both, chip, 0, keepdims=False)
    for step in range(1, chips):
        leaving = lax.dynamic_index_in_dim(both, (chip + step) % chips, 0, keepdims=False)
        pairs = [(i, (i + 2 * step) % size) for i in range(size)]
        total = total + lax.ppermute(leaving.astype(BF16), "head", pairs).astype(F32)
    return total.astype(BF16)


def per_device(
    tokens,
    region_lengths,
    header_lengths,
    w_query,
    w_key,
    w_value,
    w_gate,
    w_decay,
    w_beta,
    conv_query,
    conv_key,
    conv_value,
    decay_rate,
    decay_bias,
    beta_bias,
    norm_gain,
    w_out,
):
    seqs, tok, _ = tokens.shape
    dim = norm_gain.shape[0]
    heads = w_decay.shape[1]
    groups = w_query.shape[1] // dim
    share = heads // groups
    chunks = tok // CHUNK
    width = groups * dim
    w_small = jnp.concatenate([w_decay, w_beta], axis=1)
    places = jnp.arange(CHUNK)
    below = (places[:, None] >= places[None, :]).astype(F32)

    def one(seq, earlier):
        raw = lax.all_gather(tokens[seq], "head", axis=1, tiled=True)
        if earlier is not None:
            raw, _ = lax.optimization_barrier((raw, earlier))
        whole = augment(raw, region_lengths[seq], header_lengths[seq])

        def project(weight):
            return jnp.dot(whole, weight, preferred_element_type=F32)

        raws = [project(weight).astype(BF16) for weight in (w_query, w_key, w_value)]
        rim = shifted(jnp.concatenate([raw[tok - 3 :, :] for raw in raws], axis=-1), "ctx", 1)
        gate_raw = project(w_gate).astype(BF16)
        small = project(w_small)
        log_decay = -decay_rate * jax.nn.softplus(small[:, :heads] + decay_bias)
        strength = jax.nn.sigmoid(small[:, heads:] + beta_bias)
        cumul = jnp.einsum(
            "ij,cjh->cih", below, log_decay.reshape(chunks, CHUNK, heads), precision=HIGH
        ).reshape(tok, groups, share)
        strength = strength.reshape(tok, groups, share)
        cols = jnp.concatenate([cumul, strength], axis=-1).transpose(1, 0, 2)
        rows = cumul.transpose(1, 2, 0)
        rim = jnp.pad(rim.astype(F32), ((5, 0), (0, 0)))
        rims = (rim[:, :width], rim[:, width : 2 * width], rim[:, 2 * width :])
        maps, query_total, base_total = delta_local(
            *raws, rims, (conv_query, conv_key, conv_value), cols, rows, dim
        )
        states = incoming_states(maps, dim)
        hidden = finish(query_total, base_total, gate_raw, states, norm_gain)
        return head_sum(hidden, w_out), maps

    mixed, earlier = [], None
    for seq in range(seqs):
        result, earlier = one(seq, earlier)
        mixed.append(result)
    return jnp.stack(mixed)


def solution(mesh):
    return jax.shard_map(
        per_device,
        mesh=mesh,
        in_specs=(
            P(None, "ctx", "head"),
            P(),
            P(),
            P(None, "head"),
            P(None, "head"),
            P(None, "head"),
            P(None, "head"),
            P(None, "head"),
            P(None, "head"),
            P(None, "head"),
            P(None, "head"),
            P(None, "head"),
            P("head"),
            P("head"),
            P("head"),
            P(),
            P("head", None),
        ),
        out_specs=P(None, ("ctx", "head"), None),
        check_vma=False,
    )
```

```python
import jax
import jax.numpy as jnp
from jax import lax
from jax.experimental import pallas as pl
from jax.experimental.pallas import tpu as pltpu
from jax.sharding import PartitionSpec as P

CHUNK = 128
HIGH = lax.Precision.HIGHEST
BF16 = jnp.bfloat16
F32 = jnp.float32


def shifted(shard, axis, by):
    length = lax.axis_size(axis)
    pairs = [(i, i + by) for i in range(length) if 0 <= i + by < length]
    return lax.ppermute(shard, axis, pairs)


def dot(left, right):
    return jnp.dot(left.astype(BF16), right.astype(BF16), preferred_element_type=F32)


def silu(x):
    return x * (0.5 + 0.5 * jnp.tanh(0.5 * x))


def unit_inverses(lowers):
    size = lowers[0].shape[0]
    row = lax.broadcasted_iota(jnp.int32, (size, size), 0)
    col = lax.broadcasted_iota(jnp.int32, (size, size), 1)
    eye = (row == col).astype(F32)
    pair = (row // 2 == col // 2).astype(F32)
    inverses = [eye - pair * lower for lower in lowers]
    half = 2
    while half < size:
        below = ((row // (2 * half) == col // (2 * half)) & (row // half != col // half)).astype(F32)
        halves = [inverse.astype(BF16) for inverse in inverses]
        inner = [dot(lower * below, inverse) for lower, inverse in zip(lowers, halves)]
        outer = [dot(inverse, term) for inverse, term in zip(halves, inner)]
        inverses = [inverse - term for inverse, term in zip(inverses, outer)]
        half *= 2
    return inverses


def delta_kernel(
    q_ref, k_ref, v_ref, rq_ref, rk_ref, rv_ref, tq_ref, tk_ref, tv_ref, col_ref, row_ref,
    state_ref, query_ref, base_ref, scr,
):
    tok, dim = q_ref.shape
    share = v_ref.shape[1] // dim
    chunks = tok // CHUNK

    def conv(raw_ref, rim_ref, taps_ref, which):
        lanes = slice(which * dim, (which + 1) * dim)
        scr[0:8, :] = rim_ref[:, lanes]
        scr[8 : 8 + tok, :] = raw_ref[:, lanes].astype(F32)
        total = taps_ref[0:1, lanes] * scr[5 : 5 + tok, :]
        for i in range(1, 4):
            total = total + taps_ref[i : i + 1, lanes] * scr[5 + i : 5 + i + tok, :]
        return silu(total)

    queries = conv(q_ref, rq_ref, tq_ref, 0)
    queries = queries * (
        lax.rsqrt(jnp.sum(queries * queries, axis=-1, keepdims=True) + 1e-06) * dim ** (-0.5)
    )
    keys = conv(k_ref, rk_ref, tk_ref, 0)
    keys = keys * lax.rsqrt(jnp.sum(keys * keys, axis=-1, keepdims=True) + 1e-06)
    values = [conv(v_ref, rv_ref, tv_ref, j) for j in range(share)]

    row = lax.broadcasted_iota(jnp.int32, (CHUNK, CHUNK), 0)
    col = lax.broadcasted_iota(jnp.int32, (CHUNK, CHUNK), 1)
    incl = row >= col
    strict = row > col
    units = [(c, j) for c in range(chunks) for j in range(share)]
    lowers, attends, rights, sides, tails, decays = [], [], [], [], [], []
    for c in range(chunks):
        span = slice(c * CHUNK, (c + 1) * CHUNK)
        qc = queries[span]
        kc = keys[span]
        both = jnp.concatenate([qc, kc], axis=0).astype(BF16)
        kt = kc.T
        gram = dot(both, kt)
        for j in range(share):
            cc = col_ref[0, span, j : j + 1]
            bc = col_ref[0, span, share + j : share + j + 1]
            cr = row_ref[0, j : j + 1, span]
            last = row_ref[0, j : j + 1, (c + 1) * CHUNK - 1 : (c + 1) * CHUNK]
            ratio = jnp.where(incl, jnp.exp(jnp.minimum(cc - cr, 0.0)), 0.0)
            lowers.append(jnp.where(strict, ratio * gram[CHUNK:] * bc, 0.0))
            scaled = jnp.exp(cc)
            rights.append(
                jnp.concatenate([bc * values[j][span], (bc * scaled) * kc], axis=1).astype(BF16)
            )
            attends.append(
                jnp.concatenate([ratio * gram[:CHUNK], jnp.exp(last - cr) * kt], axis=0).astype(BF16)
            )
            sides.append((scaled * qc).astype(BF16))
            decays.append(jnp.exp(last))
    inverses = unit_inverses(lowers)
    solved = [dot(inverse, right) for inverse, right in zip(inverses, rights)]

    eye = (row == col).astype(F32)
    zero = jnp.zeros((CHUNK, dim), F32)
    states = [jnp.concatenate([eye, zero], axis=1) for _ in range(share)]
    for c in range(chunks):
        span = slice(c * CHUNK, (c + 1) * CHUNK)
        for j in range(share):
            u = c * share + j
            local = solved[u][:, :dim]
            left = jnp.concatenate([solved[u][:, dim:].astype(BF16), sides[u]], axis=0)
            seen = dot(left, states[j])
            delta = jnp.concatenate([zero, local], axis=1) - seen[:CHUNK]
            moved = dot(attends[u], delta)
            out = seen[CHUNK:] + moved[:CHUNK]
            states[j] = decays[u] * states[j] + moved[CHUNK:]
            lanes = slice(j * dim, (j + 1) * dim)
            query_ref[span, lanes] = out[:, :dim].astype(BF16)
            base_ref[span, lanes] = out[:, dim:]
    for j in range(share):
        state_ref[j] = states[j].astype(BF16)


def delta_local(q, k, v, rims, taps, cols, rows, dim):
    tok, qk_width = q.shape
    groups = qk_width // dim
    share = v.shape[1] // qk_width
    wide = share * dim
    narrow = pl.BlockSpec((tok, dim), lambda g: (0, g))
    broad = pl.BlockSpec((tok, wide), lambda g: (0, g))
    return pl.pallas_call(
        delta_kernel,
        grid=(groups,),
        in_specs=[
            narrow,
            narrow,
            broad,
            pl.BlockSpec((8, dim), lambda g: (0, g)),
            pl.BlockSpec((8, dim), lambda g: (0, g)),
            pl.BlockSpec((8, wide), lambda g: (0, g)),
            pl.BlockSpec((4, dim), lambda g: (0, g)),
            pl.BlockSpec((4, dim), lambda g: (0, g)),
            pl.BlockSpec((4, wide), lambda g: (0, g)),
            pl.BlockSpec((1, tok, 2 * share), lambda g: (g, 0, 0)),
            pl.BlockSpec((1, share, tok), lambda g: (g, 0, 0)),
        ],
        out_specs=[
            pl.BlockSpec((share, dim, 2 * dim), lambda g: (g, 0, 0)),
            broad,
            broad,
        ],
        out_shape=[
            jax.ShapeDtypeStruct((groups * share, dim, 2 * dim), BF16),
            jax.ShapeDtypeStruct(v.shape, BF16),
            jax.ShapeDtypeStruct(v.shape, F32),
        ],
        scratch_shapes=[pltpu.VMEM((tok + 8, dim), F32)],
        compiler_params=pltpu.CompilerParams(vmem_limit_bytes=48 << 20),
        cost_estimate=pl.CostEstimate(
            flops=300 * tok * v.shape[1] * dim, bytes_accessed=8 << 20, transcendentals=0
        ),
    )(q, k, v, *rims, *taps, cols, rows)


def prefix_kernel(maps_ref, out_ref):
    steps, chains, dim, _ = maps_ref.shape
    states = [jnp.zeros((dim, dim), F32) for _ in range(chains)]
    for step in range(steps):
        for c in range(chains):
            out_ref[step, c] = states[c].astype(BF16)
            if step < steps - 1:
                now = maps_ref[step, c, :, :dim]
                top = states[c].astype(BF16)
                rest = states[c] - top.astype(F32)
                states[c] = maps_ref[step, c, :, dim:].astype(F32) + dot(now, top) + dot(now, rest)


def prefix_states(maps):
    steps, chains, dim, _ = maps.shape
    return pl.pallas_call(
        prefix_kernel,
        out_shape=jax.ShapeDtypeStruct((steps, chains, dim, dim), BF16),
        compiler_params=pltpu.CompilerParams(vmem_limit_bytes=24 << 20),
    )(maps)


def finish_kernel(query_ref, base_ref, gate_ref, state_ref, gain_ref, out_ref):
    dim = gain_ref.shape[1]
    for j in range(out_ref.shape[1] // dim):
        lanes = slice(j * dim, (j + 1) * dim)
        out = dot(query_ref[:, lanes], state_ref[j]) + base_ref[:, lanes]
        mean_sq = jnp.mean(out * out, axis=-1, keepdims=True)
        gate = silu(gate_ref[:, lanes].astype(F32))
        out_ref[:, lanes] = (out * lax.rsqrt(mean_sq + 1e-06) * gain_ref[...] * gate).astype(BF16)


def finish(query, base, gate, states, gain):
    tok, width = query.shape
    dim = gain.shape[0]
    share = 2
    wide = share * dim
    broad = pl.BlockSpec((tok, wide), lambda g: (0, g))
    return pl.pallas_call(
        finish_kernel,
        grid=(width // wide,),
        in_specs=[
            broad,
            broad,
            broad,
            pl.BlockSpec((share, dim, dim), lambda g: (g, 0, 0)),
            pl.BlockSpec((1, dim), lambda g: (0, 0)),
        ],
        out_specs=broad,
        out_shape=jax.ShapeDtypeStruct((tok, width), BF16),
        compiler_params=pltpu.CompilerParams(vmem_limit_bytes=48 << 20),
        cost_estimate=pl.CostEstimate(flops=1 << 31, bytes_accessed=8 << 20, transcendentals=0),
    )(query, base, gate, states, gain.reshape(1, dim))


def region_masks(lengths, headers, tok):
    position = lax.axis_index("ctx") * tok + jnp.arange(tok, dtype=jnp.int32)
    ends = jnp.cumsum(lengths)
    starts = ends - lengths
    span = jnp.minimum(headers, lengths)
    inside = (position[None, :] >= starts[:, None]) & (position[None, :] < ends[:, None])
    header = inside & (position[None, :] < (starts + span)[:, None])

    def holds(point):
        return ((starts <= point) & (point < ends))[:, None]

    return inside, header, span, holds


def header_sums(header, tokens):
    return jnp.einsum("rt,td->rd", header.astype(BF16), tokens, preferred_element_type=F32)


def boundary_sums(tokens, masks):
    seqs, tok, part = tokens.shape
    place = lax.axis_index("ctx")
    longest = tok * lax.axis_size("ctx") // 16
    hops = -(-(longest - 1) // tok)
    sums = [header_sums(masks[seq][1], tokens[seq]) for seq in range(seqs)]

    def part_at(point):
        return jnp.stack(
            [
                jnp.sum(jnp.where(masks[seq][3](point), sums[seq], 0.0), axis=0)
                for seq in range(seqs)
            ]
        )

    before = shifted(part_at((place + 1) * tok), "ctx", 1)
    for hop in range(2, hops + 1):
        before = before + shifted(part_at((place + hop) * tok), "ctx", hop)
    after = shifted(part_at(place * tok), "ctx", -1)
    size = lax.axis_size("head")
    both = jnp.concatenate([before, after])
    spread = jnp.broadcast_to(both, (size,) + both.shape)
    held = lax.all_to_all(spread, "head", 0, 0, tiled=True)
    return held.transpose(1, 0, 2).reshape(2, seqs, size * part)


def augment(tokens, masks, before, after):
    tok = tokens.shape[0]
    place = lax.axis_index("ctx")
    inside, header, span, holds = masks
    totals = (
        header_sums(header, tokens)
        + jnp.where(holds(place * tok), before[None, :], 0.0)
        + jnp.where(holds((place + 1) * tok), after[None, :], 0.0)
    )
    means = totals / span[:, None].astype(F32)
    top = means.astype(BF16)
    rest = (means - top.astype(F32)).astype(BF16)
    spread = inside.astype(BF16)
    added = jnp.einsum(
        "rt,rd->td",
        jnp.concatenate([spread, spread], axis=0),
        jnp.concatenate([top, rest], axis=0),
        preferred_element_type=F32,
    )
    return (tokens.astype(F32) + added).astype(BF16)


def incoming_states(maps, dim, first):
    heads = maps.shape[0]
    parts = lax.axis_size("ctx")
    if heads % parts == 0:
        sent = maps.reshape(parts, heads // parts, dim, 2 * dim)
        held = lax.all_to_all(sent, "ctx", 0, 0, tiled=True)
        if first is not None:
            held, _ = lax.optimization_barrier((held, first))
        states = lax.all_to_all(prefix_states(held), "ctx", 0, 0, tiled=True)
        return states.reshape(heads, dim, dim)

    def relay(counter, state):
        moved = jnp.einsum(
            "hde,hef->hdf", maps[..., :dim], state, preferred_element_type=F32
        ) + maps[..., dim:].astype(F32)
        return shifted(moved.astype(BF16), "ctx", 1)

    states = lax.fori_loop(0, parts - 1, relay, jnp.zeros((heads, dim, dim), BF16))
    return states


def core_sum(hidden, w_out):
    size = lax.axis_size("head")
    me = lax.axis_index("head")
    chips = size // 2
    core = me % 2
    rows = hidden.shape[0] // size
    cut = hidden.reshape(chips, 2, rows, hidden.shape[1])

    def half(which):
        picked = lax.dynamic_index_in_dim(cut, which, 1, keepdims=False)
        return jnp.dot(
            picked.reshape(chips * rows, hidden.shape[1]), w_out, preferred_element_type=F32
        ).astype(BF16)

    arrived = lax.ppermute(half(1 - core), "head", [(i, i ^ 1) for i in range(size)])
    both = half(core).astype(F32) + arrived.astype(F32)
    return both.reshape(chips, rows, w_out.shape[1])


def chip_sum(both):
    size = lax.axis_size("head")
    chips = size // 2
    chip = lax.axis_index("head") // 2
    total = lax.dynamic_index_in_dim(both, chip, 0, keepdims=False)
    for step in range(1, chips):
        leaving = lax.dynamic_index_in_dim(both, (chip + step) % chips, 0, keepdims=False)
        pairs = [(i, (i + 2 * step) % size) for i in range(size)]
        total = total + lax.ppermute(leaving.astype(BF16), "head", pairs).astype(F32)
    return total.astype(BF16)


def per_device(
    tokens,
    region_lengths,
    header_lengths,
    w_query,
    w_key,
    w_value,
    w_gate,
    w_decay,
    w_beta,
    conv_query,
    conv_key,
    conv_value,
    decay_rate,
    decay_bias,
    beta_bias,
    norm_gain,
    w_out,
):
    seqs, tok, _ = tokens.shape
    dim = norm_gain.shape[0]
    heads = w_decay.shape[1]
    groups = w_query.shape[1] // dim
    share = heads // groups
    chunks = tok // CHUNK
    width = groups * dim
    w_small = jnp.concatenate([w_decay, w_beta], axis=1)
    places = jnp.arange(CHUNK)
    below = (places[:, None] >= places[None, :]).astype(F32)

    masks = [region_masks(region_lengths[i], header_lengths[i], tok) for i in range(seqs)]
    carried = boundary_sums(tokens, masks)

    def one(seq, earlier):
        raw = lax.all_gather(tokens[seq], "head", axis=1, tiled=True)
        if earlier is not None:
            raw, _ = lax.optimization_barrier((raw, earlier[0]))
        whole = augment(raw, masks[seq], carried[0, seq], carried[1, seq])

        def project(weight):
            return jnp.dot(whole, weight, preferred_element_type=F32)

        raws = [project(weight).astype(BF16) for weight in (w_query, w_key, w_value)]
        rim = shifted(jnp.concatenate([raw[tok - 3 :, :] for raw in raws], axis=-1), "ctx", 1)
        gate_raw = project(w_gate).astype(BF16)
        small = project(w_small)
        log_decay = -decay_rate * jax.nn.softplus(small[:, :heads] + decay_bias)
        strength = jax.nn.sigmoid(small[:, heads:] + beta_bias)
        cumul = jnp.einsum(
            "ij,cjh->cih", below, log_decay.reshape(chunks, CHUNK, heads), precision=HIGH
        ).reshape(tok, groups, share)
        strength = strength.reshape(tok, groups, share)
        cols = jnp.concatenate([cumul, strength], axis=-1).transpose(1, 0, 2)
        rows = cumul.transpose(1, 2, 0)
        rim = jnp.pad(rim.astype(F32), ((5, 0), (0, 0)))
        rims = (rim[:, :width], rim[:, width : 2 * width], rim[:, 2 * width :])
        if earlier is not None:
            rows, _ = lax.optimization_barrier((rows, earlier[1]))
        maps, query_total, base_total = delta_local(
            *raws, rims, (conv_query, conv_key, conv_value), cols, rows, dim
        )
        states = incoming_states(maps, dim, None if earlier is None else earlier[2])
        if earlier is not None:
            states, _ = lax.optimization_barrier((states, earlier[3]))
        hidden = finish(query_total, base_total, gate_raw, states, norm_gain)
        both = core_sum(hidden, w_out)
        mixed = chip_sum(both)
        return mixed, (maps, states, both, mixed)

    mixed, earlier = [], None
    for seq in range(seqs):
        result, earlier = one(seq, earlier)
        mixed.append(result)
    return jnp.stack(mixed)


def solution(mesh):
    return jax.shard_map(
        per_device,
        mesh=mesh,
        in_specs=(
            P(None, "ctx", "head"),
            P(),
            P(),
            P(None, "head"),
            P(None, "head"),
            P(None, "head"),
            P(None, "head"),
            P(None, "head"),
            P(None, "head"),
            P(None, "head"),
            P(None, "head"),
            P(None, "head"),
            P("head"),
            P("head"),
            P("head"),
            P(),
            P("head", None),
        ),
        out_specs=P(None, ("ctx", "head"), None),
        check_vma=False,
    )
```
